128 devices in a mesh: leaf: 32 (over z_hi, y, x), blk: 4 (over z_lo, core).
Axes of the slice: x: 4, y: 4, z: 4 (z_hi: 2, z_lo: 2; z = z_hi * 2 + z_lo), core: 2. Of those that a mesh axis runs over, the one named last changes fastest.
Arguments:
- schur: bfloat16 [32, 3, 2048, 2048], P('leaf', None, 'blk'), as said below
- modes: bfloat16 [32, 3, 2048, 512], P('leaf', None, 'blk'), may hold values from -0.125 to 0.125
- counts: int32 [32, 3], P('leaf'), may hold values from 128 to 512, as said below
Outputs:
- reduced: float32 [32, 3, 512, 512], P('leaf', None, 'blk')
The draws below stay inside these ranges and needn't reach their ends.
Inputs may be any that keep to these rules, and one draw needn't show every extreme that they name: `counts`: each entry lies from 128 to 512; some subtree keeps exactly 512. Each block schur[i, k] is symmetric with a dominant positive diagonal.
All inputs are finite; a program needn't handle non-finite values.
Results may differ from the reference program's by a relative error of at most 0.0016.
Values may be sent and summed in bfloat16 or wider, within the bound.
A program may use at most 128 MiB of HBM per device.

```python
import jax
import jax.numpy as jnp
from jax import lax

M = 2048
KMAX = 512
SUB = 3
LEV = 2
N_LEAF = 32


def draw_schur(key, part):
    key = jax.random.fold_in(key, 11)
    total = N_LEAF * SUB

    def one_block(index):
        sub_key = jax.random.fold_in(key, index)
        first, second = jax.random.split(sub_key, 2)
        rough = jax.random.normal(first, (M, M), jnp.float32) * M ** (-0.5)
        sym = (rough + rough.T) * 0.5
        diag = jax.random.uniform(second, (M,), jnp.float32, 2.0, 4.0)
        eye = jnp.arange(M)[:, None] == jnp.arange(M)[None, :]
        block = jnp.where(eye, diag[:, None] + sym, sym)
        return block.astype(jnp.bfloat16)
    blocks = lax.map(one_block, jnp.arange(total, dtype=jnp.int32))
    return blocks.reshape(N_LEAF, SUB, M, M)


def draw_counts(key, part):
    key = jax.random.fold_in(key, 23)
    first, second = jax.random.split(key)
    values = jax.random.randint(first, (N_LEAF * SUB,), KMAX // 4, KMAX + 1)
    spot = jax.random.randint(second, (), 0, N_LEAF * SUB)
    values = jnp.where(jnp.arange(N_LEAF * SUB) == spot, KMAX, values)
    return values.reshape(N_LEAF, SUB).astype(jnp.int32)


def levels(stream_key, extent, pieces, smallest, largest):
    gain = 1.0
    for position, parts in pieces:
        steps = jax.random.uniform(jax.random.fold_in(jax.random.fold_in(stream_key, 6), position), (parts,), jnp.float32, smallest / len(pieces), largest / len(pieces))
        gain = gain * jnp.repeat(jnp.exp(steps), extent[position] // parts).reshape((-1,) + (1,) * (len(extent) - 1 - position))
    return gain


def noise(key, dims, width, limit, cuts=(), kind=jnp.bfloat16):
    entries = jax.random.normal(key, dims, jnp.float32) * width
    if len(cuts) > 0:
        entries = levels(key, dims, cuts, -0.22, 0.18) * entries
    return jnp.clip(entries, min=-limit, max=limit).astype(kind)


def setup_inputs(seed: int = 0) -> dict:
    keys = jax.random.split(jax.random.key(seed), 4)
    schur = draw_schur(jax.random.fold_in(keys[3], 71), 0)
    modes = noise(keys[1], (N_LEAF, SUB, M, KMAX), M ** -0.5, 0.125, ((0, 32), (2, 4)))
    counts = draw_counts(jax.random.fold_in(keys[3], 71), 0)
    return dict(schur=schur, modes=modes, counts=counts)


def reference(schur, modes, counts):
    merged = schur.astype(jnp.float32)
    for level in range(LEV):
        partner = jnp.arange(N_LEAF, dtype=jnp.int32) ^ (1 << level)
        merged = merged + merged[partner]
    merged = merged.astype(jnp.bfloat16)
    column = jnp.arange(KMAX, dtype=jnp.int32)
    keep = column[None, None, None, :] < counts[:, :, None, None]
    kept = jnp.where(keep, modes, jnp.zeros_like(modes))
    flat_merged = merged.reshape(N_LEAF * SUB, M, M)
    flat_kept = kept.reshape(N_LEAF * SUB, M, KMAX)

    def one_subtree(pair):
        block, basis = pair
        projected = jnp.dot(block, basis, preferred_element_type=jnp.float32).astype(jnp.bfloat16)
        return jnp.dot(basis.T, projected, preferred_element_type=jnp.float32)

    reduced = lax.map(one_subtree, (flat_merged, flat_kept))
    return reduced.reshape(N_LEAF, SUB, KMAX, KMAX)
```

```python
import functools

import jax
import jax.numpy as jnp
from jax import lax
from jax.experimental import pallas as pl
from jax.experimental.pallas import tpu as pltpu
from jax.sharding import PartitionSpec as P

MESH = pl.DeviceIdType.MESH
ANY = pl.BlockSpec(memory_space=pl.ANY)
F32 = jnp.float32
BF16 = jnp.bfloat16

SUB = 3
N = 512
Q = 128
RING = 4


def dot(a, b):
    return jnp.dot(a, b, preferred_element_type=F32)


def dot_rows(a, b):
    return lax.dot_general(a, b, (((0,), (0,)), ((), ())), preferred_element_type=F32)


def kernel(
    schur, modes, out,
    raw, raw_a, m, m_a, vo, vn, vz, red, red_c, red_s, red_z,
    rs_s, rs_r, a_s, a_r, ga_s, ga_r, ag_s, ag_r, v_l, v_s, v_r, r_s, r_r, o_s,
):
    leaf = lax.axis_index("leaf")
    blk = lax.axis_index("blk")
    x = lax.rem(leaf, RING)
    base = leaf - x
    z, core = blk // 2, lax.rem(blk, 2)
    right = (base + lax.rem(x + 1, RING), blk)
    left = (base + lax.rem(x + RING - 1, RING), blk)
    across = (base + lax.rem(x + 2, RING), blk)
    twin = (leaf, z * 2 + 1 - core)
    other = (leaf, (1 - z) * 2 + core)

    nxt = lax.rem(blk + 1, 4) * N
    opp = lax.rem(blk + 2, 4) * N
    own = blk * N

    def remote(src, dst, send, recv, to):
        return pltpu.make_async_remote_copy(
            src_ref=src, dst_ref=dst, send_sem=send, recv_sem=recv, device_id=to, device_id_type=MESH
        )

    def arrived(ref, sem):
        pltpu.make_async_copy(ref, ref, sem).wait()

    for k in range(SUB):
        pltpu.make_async_copy(modes.at[0, k], vo.at[k], v_l.at[k]).start()

    barrier = pltpu.get_barrier_semaphore()
    for device in (right, left, across, twin, other):
        pl.semaphore_signal(barrier, inc=1, device_id=device, device_id_type=MESH)
    pl.semaphore_wait(barrier, 5)

    def parts(k, d):
        rows = pl.ds(d * Q, Q)
        yield schur.at[0, k, rows, pl.ds(pl.multiple_of(nxt, Q), N)], (k, 0, slice(None), slice(None))
        yield (
            schur.at[0, k, rows, pl.ds(pl.multiple_of(own + d * Q, Q), N - d * Q)],
            (k, 1, slice(None), pl.ds(d * Q, N - d * Q)),
        )
        if d:
            yield (
                schur.at[0, k, rows, pl.ds(pl.multiple_of(opp, Q), d * Q)],
                (k, 1, slice(None), pl.ds(0, d * Q)),
            )

    def scatter(k):
        for d in range(RING):

            @pl.when(x == d)
            def _():
                for src, at in parts(k, d):
                    pltpu.make_async_copy(src, raw.at[(x, *at)], rs_r.at[x, k]).start()

            @pl.when(x != d)
            def _():
                for src, at in parts(k, d):
                    remote(src, raw.at[(x, *at)], rs_s.at[d, k], rs_r.at[x, k], (base + d, blk)).start()

    def scatter_a():
        for d in range(RING):
            at = z * 256 + (d // 2) * Q
            src = schur.at[
                0, :, pl.ds(pl.multiple_of(at + (d % 2) * 64, 64), 64), pl.ds(pl.multiple_of(opp + at, Q), Q)
            ]

            @pl.when(x == d)
            def _():
                pltpu.make_async_copy(src, raw_a.at[x], a_r.at[x]).start()

            @pl.when(x != d)
            def _():
                remote(src, raw_a.at[x], a_s.at[d], a_r.at[x], (base + d, blk)).start()

    def total(ref, *at):
        t = [ref[(j, *at)].astype(F32) for j in range(RING)]
        return (t[0] + t[1]) + (t[2] + t[3])

    mine = pl.ds(pl.multiple_of(x * Q, Q), Q)
    from_left = pl.ds(pl.multiple_of(lax.rem(x + RING - 1, RING) * Q, Q), Q)
    from_right = pl.ds(pl.multiple_of(lax.rem(x + 1, RING) * Q, Q), Q)
    from_across = pl.ds(pl.multiple_of(lax.rem(x + 2, RING) * Q, Q), Q)

    def merge(k):
        for j in range(RING):
            arrived(raw.at[j, k], rs_r.at[j, k])
        m[k, 0, mine, :] = total(raw, k, 0).astype(BF16)
        column = lax.broadcasted_iota(jnp.int32, (Q, N), 1) // Q
        weight = jnp.where(column == x, 0.5, 1.0)
        m[k, 1, mine, :] = (total(raw, k, 1) * weight).astype(BF16)

    def gather(k):
        return [
            remote(m.at[k, t, mine], m.at[k, t, mine], ag_s.at[k, side, t], ag_r.at[k, side, t], to)
            for t, side, to in ((0, 0, right), (1, 1, left), (1, 0, right), (0, 1, left))
        ]

    def relay(k):
        return [
            remote(m.at[k, 0, from_left], m.at[k, 0, from_left], ag_s.at[k, 0, 2], ag_r.at[k, 0, 2], right),
            remote(m.at[k, 1, from_right], m.at[k, 1, from_right], ag_s.at[k, 1, 2], ag_r.at[k, 1, 2], left),
        ]

    def start_relay(k):
        arrived(m.at[k, 0, from_left], ag_r.at[k, 0, 0])
        relay(k)[0].start()
        arrived(m.at[k, 1, from_right], ag_r.at[k, 1, 1])
        relay(k)[1].start()

    def gathered(k):
        arrived(m.at[k, 1, from_left], ag_r.at[k, 0, 1])
        arrived(m.at[k, 0, from_right], ag_r.at[k, 1, 0])
        arrived(m.at[k, 0, from_across], ag_r.at[k, 0, 2])
        arrived(m.at[k, 1, from_across], ag_r.at[k, 1, 2])

    def gather_a():
        return [
            remote(m_a.at[x], m_a.at[x], ga_s.at[i], ga_r.at[x], to) for i, to in enumerate((right, left, across))
        ]

    def to_other(k):
        return remote(modes.at[0, k], vz.at[k], v_s.at[k, 0], v_r.at[k, 0], other)

    def to_twin(k, src):
        return remote(src, vn.at[k], v_s.at[k, 1], v_r.at[k, 1], twin)

    def pass_modes(k):
        arrived(vz.at[k], v_r.at[k, 0])

        @pl.when(core == 0)
        def _():
            to_twin(k, vz.at[k]).start()

    def project(k):
        gathered(k)
        arrived(vo.at[k], v_l.at[k])
        arrived(vn.at[k], v_r.at[k, 1])
        row = lax.broadcasted_iota(jnp.int32, (N, N), 0) // Q
        column = lax.broadcasted_iota(jnp.int32, (N, N), 1) // Q
        quarter = m[k, 1]
        zero = jnp.zeros_like(quarter)
        p = dot(m[k, 0], vn[k])
        p += dot(jnp.where(column >= row, quarter, zero), vo[k])
        lone = jnp.concatenate([m_a[d, k] for d in range(RING)], axis=0)
        lone = jnp.concatenate([lone, lone], axis=0)
        lone = jnp.concatenate([lone] * 4, axis=1)
        diagonal = (column == row) & (row // 2 == z)
        p += dot(jnp.where(column < row, quarter, jnp.where(diagonal, lone, zero)), vz[k])
        p = p.astype(BF16)
        red[k] = dot_rows(vo[k], p) + dot_rows(p, vo[k])

    def slab(i, c):
        return pl.ds(pl.multiple_of((2 * i + c) * Q, Q), Q)

    def swap_cores(k):
        return [
            remote(red.at[k, slab(i, 1 - core)], red_c.at[k, i], r_s.at[k, i], r_r.at[k, i], twin) for i in range(2)
        ]

    def swap_chips(k):
        return remote(red_s.at[k], red_z.at[k], r_s.at[k, 2], r_r.at[k, 2], other)

    def add_cores(k):
        for i in range(2):
            arrived(red_c.at[k, i], r_r.at[k, i])
        red_s[k] = red[k, slab(1 - z, core), :] + red_c[k, 1 - z]
        swap_chips(k).start()
        red_c[k, z] = red[k, slab(z, core), :] + red_c[k, z]

    def finish(k):
        arrived(red_z.at[k], r_r.at[k, 2])
        red_c[k, z] = red_c[k, z] + red_z[k]
        return pltpu.make_async_copy(red_c.at[k, z], out.at[k], o_s.at[k])

    def start(copies):
        for c in copies:
            c.start()

    scatter(0)
    for k in range(SUB):
        to_other(k).start()

    @pl.when(core == 1)
    def _():
        for k in range(SUB):
            to_twin(k, modes.at[0, k]).start()

    scatter_a()
    scatter(1)
    merge(0)
    start(gather(0))
    scatter(2)
    for j in range(RING):
        arrived(raw_a.at[j], a_r.at[j])
    m_a[x] = total(raw_a).astype(BF16)
    start(gather_a())
    pass_modes(0)
    merge(1)
    start(gather(1))
    start_relay(0)
    pass_modes(1)
    for d in range(1, RING):
        arrived(m_a.at[lax.rem(x + d, RING)], ga_r.at[lax.rem(x + d, RING)])
    project(0)
    start(swap_cores(0))
    merge(2)
    start(gather(2))
    add_cores(0)
    start_relay(1)
    pass_modes(2)
    project(1)
    start(swap_cores(1))
    start_relay(2)
    add_cores(1)
    finish(0).start()
    project(2)
    start(swap_cores(2))
    finish(1).start()
    add_cores(2)
    finish(2).start()

    for k in range(SUB):
        for d in range(RING):

            @pl.when(x != d)
            def _():
                arrived(raw.at[0, k], rs_s.at[d, k])

        for c in gather(k) + relay(k) + [to_other(k), to_twin(k, vz.at[k]), *swap_cores(k), swap_chips(k)]:
            c.wait_send()
        pltpu.make_async_copy(red_c.at[k, z], out.at[k], o_s.at[k]).wait()
    for d in range(RING):

        @pl.when(x != d)
        def _():
            arrived(raw_a.at[0], a_s.at[d])

    for c in gather_a():
        c.wait_send()


def shards(schur, modes, counts):
    dma = pltpu.SemaphoreType.DMA
    reduced = pl.pallas_call(
        kernel,
        out_shape=jax.ShapeDtypeStruct((SUB, Q, N), F32),
        in_specs=[ANY, ANY],
        out_specs=ANY,
        scratch_shapes=[
            pltpu.VMEM((RING, SUB, 2, Q, N), BF16),
            pltpu.VMEM((RING, SUB, 64, Q), BF16),
            pltpu.VMEM((SUB, 2, N, N), BF16),
            pltpu.VMEM((RING, SUB, 64, Q), BF16),
            pltpu.VMEM((SUB, N, N), BF16),
            pltpu.VMEM((SUB, N, N), BF16),
            pltpu.VMEM((SUB, N, N), BF16),
            pltpu.VMEM((SUB, N, N), F32),
            pltpu.VMEM((SUB, 2, Q, N), F32),
            pltpu.VMEM((SUB, Q, N), F32),
            pltpu.VMEM((SUB, Q, N), F32),
            dma((RING, SUB)), dma((RING, SUB)),
            dma((RING,)), dma((RING,)),
            dma((3,)), dma((RING,)),
            dma((SUB, 2, 3)), dma((SUB, 2, 3)),
            dma((SUB,)), dma((SUB, 2)), dma((SUB, 2)),
            dma((SUB, 3)), dma((SUB, 3)),
            dma((SUB,)),
        ],
        compiler_params=pltpu.CompilerParams(
            collective_id=0, has_side_effects=True, vmem_limit_bytes=56 << 20
        ),
        cost_estimate=pl.CostEstimate(flops=5 * SUB * 2 * N**3, bytes_accessed=8 << 20, transcendentals=0),
        name="merge_and_project",
    )(schur, modes)
    row = lax.axis_index("blk") * Q + lax.broadcasted_iota(jnp.int32, reduced.shape, 1)
    column = lax.broadcasted_iota(jnp.int32, reduced.shape, 2)
    kept = counts[0][:, None, None]
    return jnp.where((row < kept) & (column < kept), reduced, 0.0)[None]


def solution(mesh):
    placed = (P("leaf", None, "blk", None), P("leaf", None, "blk", None), P("leaf", None))
    return jax.shard_map(
        shards, mesh=mesh, in_specs=placed, out_specs=P("leaf", None, "blk", None), check_vma=False
    )
```

```python
import jax
import jax.numpy as jnp
from jax import lax
from jax.experimental import pallas as pl
from jax.experimental.pallas import tpu as pltpu
from jax.sharding import PartitionSpec as P

MESH = pl.DeviceIdType.MESH
ANY = pl.BlockSpec(memory_space=pl.ANY)
F32 = jnp.float32
BF16 = jnp.bfloat16

SUB = 3
N = 512
Q = 128
RING = 4


def dot(a, b):
    return jnp.dot(a, b, preferred_element_type=F32)


def dot_rows(a, b):
    return lax.dot_general(a, b, (((0,), (0,)), ((), ())), preferred_element_type=F32)


def kernel(
    schur, modes, out,
    db, ob, qp, near, inbox, part, m, diag, dg, vo, vn, vz, red, red_c, red_s, red_z, last_s, last_z,
    ld, rs_s, rs_r, d_s, d_r, ag_s, ag_r, v_s, v_r, r_s, r_r, o_s,
):
    leaf = lax.axis_index("leaf")
    blk = lax.axis_index("blk")
    x = lax.rem(leaf, RING)
    base = leaf - x
    z, core = blk // 2, lax.rem(blk, 2)
    x1, x2, x3 = (lax.rem(x + i, RING) for i in (1, 2, 3))
    right, across, left = ((base + i, blk) for i in (x1, x2, x3))
    twin = (leaf, z * 2 + 1 - core)
    other = (leaf, (1 - z) * 2 + core)

    def columns(i):
        return pl.ds(pl.multiple_of(lax.rem(blk + i, 4) * N, N), N)

    def quarter(d):
        return pl.ds(pl.multiple_of(d * Q, Q), Q)

    def remote(src, dst, send, recv, to):
        return pltpu.make_async_remote_copy(
            src_ref=src, dst_ref=dst, send_sem=send, recv_sem=recv, device_id=to, device_id_type=MESH
        )

    def arrived(ref, sem):
        pltpu.make_async_copy(ref, ref, sem).wait()

    def start(*copies):
        for c in copies:
            c.start()

    def load(k):
        for i, (src, dst) in enumerate((
            (schur.at[0, k, :, columns(0)], db.at[k]),
            (schur.at[0, k, :, columns(2)], ob.at[k]),
            (schur.at[0, k, quarter(x1), columns(1)], near.at[k, 1]),
            (schur.at[0, k, quarter(x), columns(1)], near.at[k, 0]),
            (modes.at[0, k], vo.at[k]),
        )):
            pltpu.make_async_copy(src, dst, ld.at[k, i]).start()

    def raw(k):
        return (
            remote(schur.at[0, k, quarter(x2), columns(1)], inbox.at[k, 0], rs_s.at[k, 0], rs_r.at[k, 0], right),
            remote(schur.at[0, k, quarter(x3), columns(1)], inbox.at[k, 1], rs_s.at[k, 1], rs_r.at[k, 1], left),
            remote(qp.at[k, quarter(x2)], inbox.at[k, 3], rs_s.at[k, 3], rs_r.at[k, 3], left),
            remote(qp.at[k, quarter(x1)], inbox.at[k, 4], rs_s.at[k, 4], rs_r.at[k, 4], right),
        )

    def partial(k):
        return (
            remote(part.at[k, 0], inbox.at[k, 2], rs_s.at[k, 2], rs_r.at[k, 2], right),
            remote(part.at[k, 1], inbox.at[k, 5], rs_s.at[k, 5], rs_r.at[k, 5], left),
        )

    def come(k, i):
        arrived(inbox.at[k, i], rs_r.at[k, i])
        return inbox[k, i].astype(F32)

    ri = lax.broadcasted_iota(jnp.int32, (Q, Q), 0)
    ci = lax.broadcasted_iota(jnp.int32, (Q, Q), 1)

    def at(r):
        return slice(r * Q, (r + 1) * Q)

    def pack(k):
        arrived(db.at[k], ld.at[k, 0])
        arrived(ob.at[k], ld.at[k, 1])
        for r in range(4):
            if r:
                qp[k, at(r), : r * Q] = ob[k, at(r), : r * Q]
            if r < 3:
                qp[k, at(r), (r + 1) * Q :] = db[k, at(r), (r + 1) * Q :]
            if r % 2:
                a, b = ob[k, at(r // 2), at(r // 2)], ob[k, at(2 + r // 2), at(2 + r // 2)]
                qp[k, at(r), at(r)] = jnp.where(z == 0, a, b)
            else:
                qp[k, at(r), at(r)] = jnp.where(ci > ri, db[k, at(r), at(r)], db[k, at(r + 1), at(r + 1)])

    def send_diagonals():
        for k in range(SUB):
            for r in range(4):
                own = jnp.where(ri == ci, db[k, at(r), at(r)].astype(F32), 0.0)
                dg[4 * k + r : 4 * k + r + 1, :] = jnp.sum(own, axis=0, keepdims=True)
        diag[x] = dg[...].astype(BF16)
        start(*diagonals())

    def diagonals():
        return [
            remote(diag.at[x], diag.at[x], d_s.at[i], d_r.at[x], to) for i, to in enumerate((right, left, across))
        ]

    def merge_diagonals():
        for i in (x1, x2, x3):
            arrived(diag.at[i], d_r.at[i])
        t = [diag[i].astype(F32) for i in range(RING)]
        dg[...] = ((t[0] + t[1]) + (t[2] + t[3])).astype(BF16).astype(F32) * 0.5

    def add_to_partial(k):
        arrived(near.at[k, 1], ld.at[k, 2])
        part[k, 0] = (come(k, 0) + near[k, 1].astype(F32)).astype(BF16)
        partial(k)[0].start()
        part[k, 1] = (come(k, 3) + qp[k, quarter(x3), :].astype(F32)).astype(BF16)
        partial(k)[1].start()

    def merge(k):
        arrived(near.at[k, 0], ld.at[k, 3])
        m[k, 0, quarter(x), :] = (come(k, 2) + come(k, 1) + near[k, 0].astype(F32)).astype(BF16)
        gather(k, 0, 0, right).start()
        m[k, 1, quarter(x), :] = (come(k, 5) + come(k, 4) + qp[k, quarter(x), :].astype(F32)).astype(BF16)
        gather(k, 1, 1, left).start()

    def gather(k, t, side, to):
        return remote(
            m.at[k, t, quarter(x)], m.at[k, t, quarter(x)], ag_s.at[k, side, t], ag_r.at[k, side, t], to
        )

    def gather_rest(k):
        return gather(k, 1, 0, right), gather(k, 0, 1, left)

    def relay(k, t):
        rows, to = (quarter(x3), right) if t == 0 else (quarter(x1), left)
        return remote(m.at[k, t, rows], m.at[k, t, rows], ag_s.at[k, t, 2], ag_r.at[k, t, 2], to)

    def start_relay(k):
        arrived(m.at[k, 0, quarter(x3)], ag_r.at[k, 0, 0])
        relay(k, 0).start()
        arrived(m.at[k, 1, quarter(x1)], ag_r.at[k, 1, 1])
        relay(k, 1).start()

    def gathered(k):
        arrived(m.at[k, 1, quarter(x3)], ag_r.at[k, 0, 1])
        arrived(m.at[k, 0, quarter(x1)], ag_r.at[k, 1, 0])
        arrived(m.at[k, 0, quarter(x2)], ag_r.at[k, 0, 2])
        arrived(m.at[k, 1, quarter(x2)], ag_r.at[k, 1, 2])

    def to_other(k):
        return remote(modes.at[0, k], vz.at[k], v_s.at[k, 0], v_r.at[k, 0], other)

    def to_twin(k, src):
        return remote(src, vn.at[k], v_s.at[k, 1], v_r.at[k, 1], twin)

    def pass_modes(k):
        arrived(vz.at[k], v_r.at[k, 0])

        @pl.when(core == 0)
        def _():
            to_twin(k, vz.at[k]).start()

    def project(k):
        gathered(k)
        row = lax.broadcasted_iota(jnp.int32, (N, N), 0) // Q
        column = lax.broadcasted_iota(jnp.int32, (N, N), 1) // Q
        both = m[k, 1]
        zero = jnp.zeros_like(both)
        db[k] = jnp.where(column > row, both, zero)
        ob[k] = jnp.where(column < row, both, zero)
        for r in range(4):
            two = m[k, 1, at(r // 2 * 2), at(r // 2 * 2)].astype(F32)
            half = dg[4 * k + r : 4 * k + r + 1, :]
            beside = ci < ri if r % 2 else ci > ri
            db[k, at(r), at(r)] = jnp.where(ri == ci, half, jnp.where(beside, two, 0.0)).astype(BF16)
            lone = m[k, 1, at(r % 2 * 2 + 1), at(r % 2 * 2 + 1)]
            ob[k, at(r), at(r)] = jnp.where(z == r // 2, lone, jnp.zeros_like(lone))
        arrived(vo.at[k], ld.at[k, 4])
        arrived(vn.at[k], v_r.at[k, 1])
        p = (dot(m[k, 0], vn[k]) + dot(db[k], vo[k]) + dot(ob[k], vz[k])).astype(BF16)
        red[k] = dot_rows(vo[k], p) + dot_rows(p, vo[k])
        start(*swap_cores(k))

    def slab(i, c):
        return pl.ds(pl.multiple_of((2 * i + c) * Q, Q), Q)

    def swap_cores(k):
        return [
            remote(red.at[k, slab(i, 1 - core)], red_c.at[k, i], r_s.at[k, j], r_r.at[k, i], twin)
            for j, i in enumerate((1 - z, z))
        ]

    def swap_chips(k):
        src, dst = (last_s, last_z) if k == SUB - 1 else (red_s.at[k], red_z.at[k])
        return remote(src, dst, r_s.at[k, 2], r_r.at[k, 2], other)

    def add_cores(k):
        arrived(red_c.at[k, 1 - z], r_r.at[k, 1 - z])
        away = red[k, slab(1 - z, core), :] + red_c[k, 1 - z]
        if k == SUB - 1:
            last_s[...] = away.astype(BF16)
        else:
            red_s[k] = away
        swap_chips(k).start()
        arrived(red_c.at[k, z], r_r.at[k, z])
        red_c[k, z] = red[k, slab(z, core), :] + red_c[k, z]

    def finish(k):
        if k == SUB - 1:
            arrived(last_z, r_r.at[k, 2])
            red_c[k, z] = red_c[k, z] + last_z[...].astype(F32)
        else:
            arrived(red_z.at[k], r_r.at[k, 2])
            red_c[k, z] = red_c[k, z] + red_z[k]
        result(k).start()

    def result(k):
        return pltpu.make_async_copy(red_c.at[k, z], out.at[k], o_s.at[k])

    for k in range(SUB):
        load(k)

    barrier = pltpu.get_barrier_semaphore()
    for device in (right, left, across, twin, other):
        pl.semaphore_signal(barrier, inc=1, device_id=device, device_id_type=MESH)
    pl.semaphore_wait(barrier, 5)

    start(*raw(0)[:2])
    to_other(0).start()

    @pl.when(core == 1)
    def _():
        for k in range(SUB):
            to_twin(k, modes.at[0, k]).start()

    pack(0)
    start(*raw(0)[2:])
    start(*raw(1)[:2])
    to_other(1).start()
    pack(1)
    start(*raw(1)[2:])
    to_other(2).start()
    add_to_partial(0)
    start(*raw(2)[:2])
    pack(2)
    start(*raw(2)[2:])
    send_diagonals()
    add_to_partial(1)
    merge(0)
    start(*gather_rest(0))
    pass_modes(0)
    add_to_partial(2)
    start_relay(0)
    merge(1)
    start(*gather_rest(1))
    pass_modes(1)
    merge_diagonals()
    project(0)
    merge(2)
    add_cores(0)
    start_relay(1)
    start(*gather_rest(2))
    pass_modes(2)
    start_relay(2)
    finish(0)
    project(1)
    add_cores(1)
    project(2)
    add_cores(2)
    finish(1)
    finish(2)

    for k in range(SUB):
        copies = [*raw(k), *partial(k), gather(k, 0, 0, right), gather(k, 1, 1, left), *gather_rest(k)]
        copies += [relay(k, 0), relay(k, 1), to_other(k), to_twin(k, vz.at[k]), *swap_cores(k), swap_chips(k)]
        for c in copies:
            c.wait_send()
        result(k).wait()
    for c in diagonals():
        c.wait_send()


def shards(schur, modes, counts):
    dma = pltpu.SemaphoreType.DMA
    pinned = pl.BlockSpec(memory_space=pltpu.HBM)
    reduced = pl.pallas_call(
        kernel,
        out_shape=jax.ShapeDtypeStruct((SUB, Q, N), F32),
        in_specs=[pinned, pinned],
        out_specs=ANY,
        scratch_shapes=[
            pltpu.VMEM((SUB, N, N), BF16),
            pltpu.VMEM((SUB, N, N), BF16),
            pltpu.VMEM((SUB, N, N), BF16),
            pltpu.VMEM((SUB, 2, Q, N), BF16),
            pltpu.VMEM((SUB, 6, Q, N), BF16),
            pltpu.VMEM((SUB, 2, Q, N), BF16),
            pltpu.VMEM((SUB, 2, N, N), BF16),
            pltpu.VMEM((RING, 16, Q), BF16),
            pltpu.VMEM((16, Q), F32),
            pltpu.VMEM((SUB, N, N), BF16),
            pltpu.VMEM((SUB, N, N), BF16),
            pltpu.VMEM((SUB, N, N), BF16),
            pltpu.VMEM((SUB, N, N), F32),
            pltpu.VMEM((SUB, 2, Q, N), F32),
            pltpu.VMEM((SUB - 1, Q, N), F32),
            pltpu.VMEM((SUB - 1, Q, N), F32),
            pltpu.VMEM((Q, N), BF16),
            pltpu.VMEM((Q, N), BF16),
            dma((SUB, 5)),
            dma((SUB, 6)), dma((SUB, 6)),
            dma((3,)), dma((RING,)),
            dma((SUB, 2, 3)), dma((SUB, 2, 3)),
            dma((SUB, 2)), dma((SUB, 2)),
            dma((SUB, 3)), dma((SUB, 3)),
            dma((SUB,)),
        ],
        compiler_params=pltpu.CompilerParams(
            collective_id=0, has_side_effects=True, vmem_limit_bytes=52 << 20
        ),
        cost_estimate=pl.CostEstimate(flops=5 * SUB * 2 * N**3, bytes_accessed=8 << 20, transcendentals=0),
        name="merge_and_project",
    )(schur, modes)
    row = lax.axis_index("blk") * Q + lax.broadcasted_iota(jnp.int32, reduced.shape, 1)
    column = lax.broadcasted_iota(jnp.int32, reduced.shape, 2)
    kept = counts[0][:, None, None]
    return jnp.where((row < kept) & (column < kept), reduced, 0.0)[None]


def solution(mesh):
    placed = (P("leaf", None, "blk", None), P("leaf", None, "blk", None), P("leaf", None))
    return jax.shard_map(
        shards, mesh=mesh, in_specs=placed, out_specs=P("leaf", None, "blk", None), check_vma=False
    )
```

```python
import jax
import jax.numpy as jnp
from jax import lax
from jax.experimental import pallas as pl
from jax.experimental.pallas import tpu as pltpu
from jax.sharding import PartitionSpec as P

MESH = pl.DeviceIdType.MESH
ANY = pl.BlockSpec(memory_space=pl.ANY)
F32 = jnp.float32
BF16 = jnp.bfloat16

SUB = 3
N = 512
Q = 128
RING = 4


def dot(a, b):
    return jnp.dot(a, b, preferred_element_type=F32)


def dot_rows(a, b):
    return lax.dot_general(a, b, (((0,), (0,)), ((), ())), preferred_element_type=F32)


def kernel(
    schur, modes, out, out_far,
    db, ob, qp, near, inbox, part, m, diag, dg, halves, vo, vt, vz, p, late, keep, away, far, short, short_far,
    ld, rs_s, rs_r, d_s, d_r, ag_s, ag_r, v_s, v_r, p_s, p_r, r_s, r_r, o_s,
):
    leaf = lax.axis_index("leaf")
    blk = lax.axis_index("blk")
    x = lax.rem(leaf, RING)
    base = leaf - x
    z, core = blk // 2, lax.rem(blk, 2)
    x1, x2, x3 = (lax.rem(x + i, RING) for i in (1, 2, 3))
    right, across, left = ((base + i, blk) for i in (x1, x2, x3))
    twin = (leaf, z * 2 + 1 - core)
    other = (leaf, (1 - z) * 2 + core)

    def columns(i):
        return pl.ds(pl.multiple_of(lax.rem(blk + i, 4) * N, N), N)

    def quarter(d):
        return pl.ds(pl.multiple_of(d * Q, Q), Q)

    def remote(src, dst, send, recv, to):
        return pltpu.make_async_remote_copy(
            src_ref=src, dst_ref=dst, send_sem=send, recv_sem=recv, device_id=to, device_id_type=MESH
        )

    def arrived(ref, sem):
        pltpu.make_async_copy(ref, ref, sem).wait()

    def start(*copies):
        for c in copies:
            c.start()

    def load(k):
        for i, (src, dst) in enumerate((
            (schur.at[0, k, :, columns(0)], db.at[k]),
            (schur.at[0, k, :, columns(2)], ob.at[k]),
            (schur.at[0, k, quarter(x1), columns(1)], near.at[k, 1]),
            (schur.at[0, k, quarter(x), columns(1)], near.at[k, 0]),
            (modes.at[0, k], vo.at[k]),
        )):
            pltpu.make_async_copy(src, dst, ld.at[k, i]).start()

    def raw(k):
        return (
            remote(schur.at[0, k, quarter(x2), columns(1)], inbox.at[k, 0], rs_s.at[k, 0], rs_r.at[k, 0], right),
            remote(schur.at[0, k, quarter(x3), columns(1)], inbox.at[k, 1], rs_s.at[k, 1], rs_r.at[k, 1], left),
            remote(qp.at[k, quarter(x2)], inbox.at[k, 3], rs_s.at[k, 3], rs_r.at[k, 3], left),
            remote(qp.at[k, quarter(x1)], inbox.at[k, 4], rs_s.at[k, 4], rs_r.at[k, 4], right),
        )

    def partial(k):
        return (
            remote(part.at[k, 0], inbox.at[k, 2], rs_s.at[k, 2], rs_r.at[k, 2], right),
            remote(part.at[k, 1], inbox.at[k, 5], rs_s.at[k, 5], rs_r.at[k, 5], left),
        )

    def come(k, i):
        arrived(inbox.at[k, i], rs_r.at[k, i])
        return inbox[k, i].astype(F32)

    def places(blocks):
        row = jnp.concatenate([lax.broadcasted_iota(jnp.int32, (Q, N), 0) + d * Q for d in blocks], axis=0)
        return row, lax.broadcasted_iota(jnp.int32, row.shape, 1)

    def pack(k):
        arrived(db.at[k], ld.at[k, 0])
        arrived(ob.at[k], ld.at[k, 1])
        row, column = places(range(4))
        qp[k] = jnp.where(column > row, db[k], ob[k])

    def send_diagonals():
        row = lax.broadcasted_iota(jnp.int32, (Q, Q), 0)
        column = lax.broadcasted_iota(jnp.int32, (Q, Q), 1)
        for k in range(SUB):
            for r in range(4):
                own = db[k, r * Q : (r + 1) * Q, r * Q : (r + 1) * Q].astype(F32)
                dg[4 * k + r : 4 * k + r + 1, :] = jnp.sum(jnp.where(row == column, own, 0.0), axis=0, keepdims=True)
        diag[x] = dg[...].astype(BF16)
        start(*diagonals())

    def diagonals():
        return [
            remote(diag.at[x], diag.at[x], d_s.at[i], d_r.at[x], to) for i, to in enumerate((right, left, across))
        ]

    def merge_diagonals():
        for i in (x1, x2, x3):
            arrived(diag.at[i], d_r.at[i])
        t = [diag[i].astype(F32) for i in range(RING)]
        dg[...] = ((t[0] + t[1]) + (t[2] + t[3])).astype(BF16).astype(F32) * 0.5
        for k in range(SUB):
            for r in range(4):
                halves[k : k + 1, r * Q : (r + 1) * Q] = dg[4 * k + r : 4 * k + r + 1, :]

    def add_to_partial(k, t):
        if t == 0:
            arrived(near.at[k, 1], ld.at[k, 2])
            part[k, 0] = (come(k, 0) + near[k, 1].astype(F32)).astype(BF16)
        else:
            part[k, 1] = (come(k, 3) + qp[k, quarter(x3), :].astype(F32)).astype(BF16)
        partial(k)[t].start()

    def merge(k, t):
        if t == 0:
            arrived(near.at[k, 0], ld.at[k, 3])
            m[k, 0, quarter(x), :] = (come(k, 2) + come(k, 1) + near[k, 0].astype(F32)).astype(BF16)
        else:
            m[k, 1, quarter(x), :] = (come(k, 5) + come(k, 4) + qp[k, quarter(x), :].astype(F32)).astype(BF16)
        gather_first(k)[t].start()

    def gather_first(k):
        return gather(k, 0, 0, right), gather(k, 1, 1, left)

    def gather(k, t, side, to):
        return remote(
            m.at[k, t, quarter(x)], m.at[k, t, quarter(x)], ag_s.at[k, side, t], ag_r.at[k, side, t], to
        )

    def gather_rest(k):
        return gather(k, 1, 0, right), gather(k, 0, 1, left)

    def relay(k, t):
        rows, to = (quarter(x3), right) if t == 0 else (quarter(x1), left)
        return remote(m.at[k, t, rows], m.at[k, t, rows], ag_s.at[k, t, 2], ag_r.at[k, t, 2], to)

    def start_relay(k, t):
        arrived(m.at[k, t, quarter(x1 if t else x3)], ag_r.at[k, t, t])
        relay(k, t).start()

    def gathered_near(k):
        arrived(m.at[k, 1, quarter(x3)], ag_r.at[k, 0, 1])
        arrived(m.at[k, 0, quarter(x1)], ag_r.at[k, 1, 0])

    def gathered_far(k):
        for t in range(2):
            arrived(m.at[k, t, quarter(x2)], ag_r.at[k, t, 2])

    def to_other(k):
        return remote(modes.at[0, k], vz.at[k], v_s.at[k, 0], v_r.at[k, 0], other)

    def to_twin(k):
        return remote(modes.at[0, k], vt.at[k, 0], v_s.at[k, 1], v_r.at[k, 1], twin)

    def on_to_twin(k):
        return remote(vz.at[k], vt.at[k, 1], v_s.at[k, 2], v_r.at[k, 2], twin)

    def pass_modes(k):
        arrived(vz.at[k], v_r.at[k, 0])

        @pl.when(core == 0)
        def _():
            on_to_twin(k).start()

    def modes_here(k):
        arrived(vo.at[k], ld.at[k, 4])
        arrived(vt.at[k, 0], v_r.at[k, 1])

        @pl.when(core == 1)
        def _():
            arrived(vt.at[k, 1], v_r.at[k, 2])

    def upper(k, blocks, both):
        row, column = places(blocks)
        zero = jnp.zeros_like(both)
        half = jnp.broadcast_to(halves[k : k + 1, :], both.shape).astype(BF16)
        own = jnp.where(column > row, both, jnp.where(column == row, half, zero))
        opposite = jnp.where(column < row, both, jnp.where(column == row, both * 0.5, zero))
        return own, opposite

    def project(k, blocks, following, both):
        own, opposite = upper(k, blocks, both)
        return (dot(following, vt[k, core]) + dot(own, vo[k]) + dot(opposite, vz[k])).astype(BF16)

    def project_blocks(k, *blocks):
        following, both = (jnp.concatenate([m[k, t, quarter(d), :] for d in blocks], axis=0) for t in range(2))
        return project(k, blocks, following, both)

    def swap(k):
        return remote(p.at[k, 0], p.at[k, 1], p_s.at[k], p_r.at[k], twin)

    def swap_late():
        return remote(late.at[0], late.at[1], p_s.at[SUB], p_r.at[SUB], twin)

    def project_all(k):
        gathered_near(k)
        gathered_far(k)
        modes_here(k)
        p[k, 0] = project(k, range(4), m[k, 0], m[k, 1])
        swap(k).start()

    def project_mine(k):
        modes_here(k)
        p[k, 0, quarter(x), :] = project_blocks(k, x)
        p[k, 0, quarter(x2), :] = jnp.zeros((Q, N), BF16)

    def project_sides(k):
        gathered_near(k)
        sides = project_blocks(k, x1, x3)
        p[k, 0, quarter(x1), :] = sides[:Q]
        p[k, 0, quarter(x3), :] = sides[Q:]
        swap(k).start()

    def project_far(k):
        gathered_far(k)
        late[0] = project_blocks(k, x2)
        swap_late().start()

    def slab(i):
        return pl.ds(pl.multiple_of((2 * i + core) * Q, Q), Q)

    def reduced(k, i):
        total = dot_rows(vo[k, :, slab(i)], p[k, 0]) + dot_rows(p[k, 0, :, slab(i)], vo[k])
        return total + dot_rows(vt[k, 0, :, slab(i)], p[k, 1]) + dot_rows(p[k, 1, :, slab(i)], vt[k, 0])

    def reduced_late(k, i):
        total = dot_rows(vo[k, quarter(x2), slab(i)], late[0]) + dot_rows(late[0, :, slab(i)], vo[k, quarter(x2), :])
        total += dot_rows(vt[k, 0, quarter(x2), slab(i)], late[1])
        return total + dot_rows(late[1, :, slab(i)], vt[k, 0, quarter(x2), :])

    def swap_chips(k):
        if k == SUB - 1:
            return remote(short.at[1], out_far, r_s.at[k], r_r.at[k], other)
        if k:
            return remote(short.at[0], short_far, r_s.at[k], r_r.at[k], other)
        return remote(away.at[0], far, r_s.at[k], r_r.at[k], other)

    def reduce_away(k):
        arrived(p.at[k, 1], p_r.at[k])
        away[k] = reduced(k, 1 - z)
        if k == 1:
            short[0] = away[k].astype(BF16)
        if k < SUB - 1:
            swap_chips(k).start()

    def reduce_keep(k):
        keep[k] = reduced(k, z)

    def late_away(k):
        arrived(late.at[1], p_r.at[SUB])
        short[1] = (away[k] + reduced_late(k, 1 - z)).astype(BF16)
        swap_chips(k).start()

    def late_keep(k):
        keep[k] = keep[k] + reduced_late(k, z)
        result(k).start()

    def finish(k):
        there = short_far if k else far
        arrived(there, r_r.at[k])
        keep[k] = keep[k] + there[...].astype(F32)
        result(k).start()

    def result(k):
        return pltpu.make_async_copy(keep.at[k], out.at[k], o_s.at[k])

    for k in range(SUB):
        load(k)

    barrier = pltpu.get_barrier_semaphore()
    for device in (right, left, across, twin, other):
        pl.semaphore_signal(barrier, inc=1, device_id=device, device_id_type=MESH)
    pl.semaphore_wait(barrier, 5)

    start(*raw(0)[:2])
    start(to_other(0), to_twin(0))
    start(to_other(1), to_twin(1))
    start(to_other(2), to_twin(2))
    pack(0)
    start(*raw(0)[2:])
    start(*raw(1)[:2])
    pack(1)
    start(*raw(1)[2:])
    add_to_partial(0, 0)
    add_to_partial(0, 1)
    pack(2)
    send_diagonals()
    add_to_partial(1, 0)
    add_to_partial(1, 1)
    merge(0, 0)
    merge(0, 1)
    start(*gather_rest(0))
    start(*raw(2)[:2])
    start(*raw(2)[2:])
    merge(1, 0)
    merge(1, 1)
    start(*gather_rest(1))
    start_relay(0, 0)
    start_relay(0, 1)
    pass_modes(0)
    merge_diagonals()
    add_to_partial(2, 0)
    add_to_partial(2, 1)
    pass_modes(1)
    start_relay(1, 0)
    start_relay(1, 1)
    project_all(0)
    merge(2, 0)
    merge(2, 1)
    start(*gather_rest(2))
    reduce_away(0)
    reduce_keep(0)
    pass_modes(2)
    project_all(1)
    start_relay(2, 0)
    start_relay(2, 1)
    reduce_away(1)
    reduce_keep(1)
    project_mine(2)
    project_sides(2)
    finish(0)
    reduce_away(2)
    reduce_keep(2)
    project_far(2)
    late_away(2)
    late_keep(2)
    finish(1)
    arrived(out_far, r_r.at[SUB - 1])

    for k in range(SUB):
        copies = [*raw(k), *partial(k), *gather_first(k), *gather_rest(k)]
        copies += [relay(k, 0), relay(k, 1), to_other(k), to_twin(k), swap(k), swap_chips(k)]
        for c in copies:
            c.wait_send()
        result(k).wait()
    for c in (*diagonals(), swap_late()):
        c.wait_send()

    @pl.when(core == 0)
    def _():
        for k in range(SUB):
            on_to_twin(k).wait_send()


def shards(schur, modes, counts):
    dma = pltpu.SemaphoreType.DMA
    reduced, far = pl.pallas_call(
        kernel,
        out_shape=(jax.ShapeDtypeStruct((SUB, Q, N), F32), jax.ShapeDtypeStruct((Q, N), BF16)),
        in_specs=[ANY, ANY],
        out_specs=(ANY, ANY),
        scratch_shapes=[
            pltpu.VMEM((SUB, N, N), BF16),
            pltpu.VMEM((SUB, N, N), BF16),
            pltpu.VMEM((SUB, N, N), BF16),
            pltpu.VMEM((SUB, 2, Q, N), BF16),
            pltpu.VMEM((SUB, 6, Q, N), BF16),
            pltpu.VMEM((SUB, 2, Q, N), BF16),
            pltpu.VMEM((SUB, 2, N, N), BF16),
            pltpu.VMEM((RING, 16, Q), BF16),
            pltpu.VMEM((16, Q), F32),
            pltpu.VMEM((8, N), F32),
            pltpu.VMEM((SUB, N, N), BF16),
            pltpu.VMEM((SUB, 2, N, N), BF16),
            pltpu.VMEM((SUB, N, N), BF16),
            pltpu.VMEM((SUB, 2, N, N), BF16),
            pltpu.VMEM((2, Q, N), BF16),
            pltpu.VMEM((SUB, Q, N), F32),
            pltpu.VMEM((SUB, Q, N), F32),
            pltpu.VMEM((Q, N), F32),
            pltpu.VMEM((2, Q, N), BF16),
            pltpu.VMEM((Q, N), BF16),
            dma((SUB, 5)),
            dma((SUB, 6)), dma((SUB, 6)),
            dma((3,)), dma((RING,)),
            dma((SUB, 2, 3)), dma((SUB, 2, 3)),
            dma((SUB, 3)), dma((SUB, 3)),
            dma((SUB + 1,)), dma((SUB + 1,)),
            dma((SUB,)), dma((SUB,)),
            dma((SUB,)),
        ],
        compiler_params=pltpu.CompilerParams(
            collective_id=0, has_side_effects=True, vmem_limit_bytes=52 << 20
        ),
        cost_estimate=pl.CostEstimate(flops=5 * SUB * 2 * N**3, bytes_accessed=8 << 20, transcendentals=0),
        name="merge_and_project",
    )(schur, modes)
    reduced += jnp.pad(far.astype(F32)[None], ((SUB - 1, 0), (0, 0), (0, 0)))
    row = lax.axis_index("blk") * Q + lax.broadcasted_iota(jnp.int32, reduced.shape, 1)
    column = lax.broadcasted_iota(jnp.int32, reduced.shape, 2)
    kept = counts[0][:, None, None]
    return jnp.where((row < kept) & (column < kept), reduced, 0.0)[None]


def solution(mesh):
    placed = (P("leaf", None, "blk", None), P("leaf", None, "blk", None), P("leaf", None))
    return jax.shard_map(
        shards, mesh=mesh, in_specs=placed, out_specs=P("leaf", None, "blk", None), check_vma=False
    )
```

```python
import jax
import jax.numpy as jnp
from jax import lax
from jax.experimental import pallas as pl
from jax.experimental.pallas import tpu as pltpu
from jax.sharding import PartitionSpec as P

MESH = pl.DeviceIdType.MESH
ANY = pl.BlockSpec(memory_space=pl.ANY)
F32 = jnp.float32
BF16 = jnp.bfloat16

SUB = 3
N = 512
Q = 128
RING = 4


def dot(a, b):
    return jnp.dot(a, b, preferred_element_type=F32)


def dot_rows(a, b):
    return lax.dot_general(a, b, (((0,), (0,)), ((), ())), preferred_element_type=F32)


def kernel(
    schur, modes, out, out_far,
    db, ob, qp, near, inbox, part, m, diag, dg, halves, vo, vt, vz, p, late, keep, away, far, short, short_far,
    load_sem, sent, raw_sem, diag_sem, all_sem, modes_sem, swap_sem, chip_sem, out_sem,
):
    leaf = lax.axis_index("leaf")
    blk = lax.axis_index("blk")
    x = lax.rem(leaf, RING)
    base = leaf - x
    z, core = blk // 2, lax.rem(blk, 2)
    x1, x2, x3 = (lax.rem(x + i, RING) for i in (1, 2, 3))
    right, across, left = ((base + i, blk) for i in (x1, x2, x3))
    twin = (leaf, z * 2 + 1 - core)
    other = (leaf, (1 - z) * 2 + core)

    def columns(i):
        return pl.ds(pl.multiple_of(lax.rem(blk + i, 4) * N, N), N)

    def quarter(d):
        return pl.ds(pl.multiple_of(d * Q, Q), Q)

    def remote(src, dst, send, recv, to):
        return pltpu.make_async_remote_copy(
            src_ref=src, dst_ref=dst, send_sem=send, recv_sem=recv, device_id=to, device_id_type=MESH
        )

    def arrived(ref, sem):
        pltpu.make_async_copy(ref, ref, sem).wait()

    def start(*copies):
        for c in copies:
            c.start()

    def load():
        for k in range(SUB):
            for i, dst in ((0, db), (2, ob)):
                pltpu.make_async_copy(schur.at[0, k, :, columns(i)], dst.at[k], load_sem.at[k]).start()
        for i, d in enumerate((x, x1)):
            pltpu.make_async_copy(schur.at[0, :, quarter(d), columns(1)], near.at[:, i], load_sem.at[SUB]).start()
        pltpu.make_async_copy(modes.at[0], vo, load_sem.at[SUB + 1]).start()

    def raw(k, t):
        def send(i, d, sem, to):
            src = qp.at[k, quarter(d)] if t else schur.at[0, k, quarter(d), columns(1)]
            return remote(src, inbox.at[k, i], sent.at[0], raw_sem.at[k, sem], to)

        if t:
            return send(3, x2, 2, left), send(4, x1, 3, right)
        return send(0, x2, 0, right), send(1, x3, 1, left)

    def partial(k, t):
        dst = inbox.at[k, 5 if t else 2]
        return remote(part.at[k, t], dst, sent.at[1], raw_sem.at[k, 3 if t else 1], left if t else right)

    def places(blocks):
        row = jnp.concatenate([lax.broadcasted_iota(jnp.int32, (Q, N), 0) + d * Q for d in blocks], axis=0)
        return row, lax.broadcasted_iota(jnp.int32, row.shape, 1)

    def pack(k):
        arrived(p.at[k], load_sem.at[k])
        row, column = places(range(4))
        qp[k] = jnp.where(column > row, db[k], ob[k])

    def send_diagonals():
        row = lax.broadcasted_iota(jnp.int32, (Q, Q), 0)
        column = lax.broadcasted_iota(jnp.int32, (Q, Q), 1)
        for k in range(SUB):
            for r in range(4):
                own = db[k, r * Q : (r + 1) * Q, r * Q : (r + 1) * Q].astype(F32)
                dg[4 * k + r : 4 * k + r + 1, :] = jnp.sum(jnp.where(row == column, own, 0.0), axis=0, keepdims=True)
        diag[x] = dg[...].astype(BF16)
        start(*diagonals())

    def diagonals():
        return [remote(diag.at[x], diag.at[x], sent.at[2], diag_sem, to) for to in (right, left, across)]

    def merge_diagonals():
        arrived(diag.at[pl.ds(0, 3)], diag_sem)
        t = [diag[i].astype(F32) for i in range(RING)]
        dg[...] = ((t[0] + t[1]) + (t[2] + t[3])).astype(BF16).astype(F32) * 0.5
        for k in range(SUB):
            for r in range(4):
                halves[k : k + 1, r * Q : (r + 1) * Q] = dg[4 * k + r : 4 * k + r + 1, :]

    def add_to_partial(k, t):
        arrived(inbox.at[k, 3 * t], raw_sem.at[k, 2 * t])
        own = qp[k, quarter(x3), :] if t else near[k, 1]
        part[k, t] = (inbox[k, 3 * t].astype(F32) + own.astype(F32)).astype(BF16)
        partial(k, t).start()

    def merge(k, t):
        two = pl.ds(3 * t + 1, 2)
        arrived(inbox.at[k, two], raw_sem.at[k, 2 * t + 1])
        own = qp[k, quarter(x), :] if t else near[k, 0]
        total = inbox[k, 3 * t + 2].astype(F32) + inbox[k, 3 * t + 1].astype(F32) + own.astype(F32)
        m[k, t, quarter(x), :] = total.astype(BF16)
        gather(k, t, t, t).start()

    def gather(k, t, side, sem):
        ref = m.at[k, t, quarter(x)]
        return remote(ref, ref, sent.at[0], all_sem.at[k, sem], left if side else right)

    def gather_rest(k):
        return gather(k, 1, 0, 2), gather(k, 0, 1, 2)

    def start_relay(k, t):
        ref = m.at[k, t, quarter(x1 if t else x3)]
        arrived(ref, all_sem.at[k, t])
        remote(ref, ref, sent.at[1], all_sem.at[k, 3], left if t else right).start()

    def gathered_near(k):
        arrived(inbox.at[k, pl.ds(0, 2)], all_sem.at[k, 2])

    def gathered_far(k):
        arrived(inbox.at[k, pl.ds(0, 2)], all_sem.at[k, 3])

    def to_other(k):
        return remote(modes.at[0, k], vz.at[k], sent.at[3], modes_sem.at[k], other)

    def to_twin():
        return remote(modes.at[0], vt.at[:, 0], sent.at[3], modes_sem.at[SUB], twin)

    def pass_modes(k):
        arrived(vz.at[k], modes_sem.at[k])

        @pl.when(core == 0)
        def _():
            remote(vz.at[k], vt.at[k, 1], sent.at[4], modes_sem.at[SUB + 1 + k], twin).start()

    def modes_here(k):
        @pl.when(core == 1)
        def _():
            arrived(vt.at[k, 1], modes_sem.at[SUB + 1 + k])

    def upper(k, blocks, both):
        row, column = places(blocks)
        zero = jnp.zeros_like(both)
        half = jnp.broadcast_to(halves[k : k + 1, :], both.shape).astype(BF16)
        own = jnp.where(column > row, both, jnp.where(column == row, half, zero))
        opposite = jnp.where(column < row, both, jnp.where(column == row, both * 0.5, zero))
        return own, opposite

    def project(k, blocks, following, both):
        own, opposite = upper(k, blocks, both)
        return (dot(following, vt[k, core]) + dot(own, vo[k]) + dot(opposite, vz[k])).astype(BF16)

    def project_blocks(k, *blocks):
        following, both = (jnp.concatenate([m[k, t, quarter(d), :] for d in blocks], axis=0) for t in range(2))
        return project(k, blocks, following, both)

    def swap(k):
        return remote(p.at[k, 0], p.at[k, 1], sent.at[5], swap_sem.at[k], twin)

    def swap_late():
        return remote(late.at[0], late.at[1], sent.at[6], swap_sem.at[SUB], twin)

    def project_all(k):
        gathered_near(k)
        gathered_far(k)
        modes_here(k)
        p[k, 0] = project(k, range(4), m[k, 0], m[k, 1])
        swap(k).start()

    def project_mine(k):
        modes_here(k)
        p[k, 0, quarter(x), :] = project_blocks(k, x)
        p[k, 0, quarter(x2), :] = jnp.zeros((Q, N), BF16)

    def project_sides(k):
        gathered_near(k)
        sides = project_blocks(k, x1, x3)
        p[k, 0, quarter(x1), :] = sides[:Q]
        p[k, 0, quarter(x3), :] = sides[Q:]
        swap(k).start()

    def project_far(k):
        gathered_far(k)
        late[0] = project_blocks(k, x2)
        swap_late().start()

    def slab(i):
        return pl.ds(pl.multiple_of((2 * i + core) * Q, Q), Q)

    def reduced(k, i):
        total = dot_rows(vo[k, :, slab(i)], p[k, 0]) + dot_rows(p[k, 0, :, slab(i)], vo[k])
        return total + dot_rows(vt[k, 0, :, slab(i)], p[k, 1]) + dot_rows(p[k, 1, :, slab(i)], vt[k, 0])

    def reduced_late(k, i):
        total = dot_rows(vo[k, quarter(x2), slab(i)], late[0]) + dot_rows(late[0, :, slab(i)], vo[k, quarter(x2), :])
        total += dot_rows(vt[k, 0, quarter(x2), slab(i)], late[1])
        return total + dot_rows(late[1, :, slab(i)], vt[k, 0, quarter(x2), :])

    def swap_chips(k):
        src, dst = ((away.at[0], far), (short.at[0], short_far), (short.at[1], out_far))[k]
        return remote(src, dst, sent.at[6], chip_sem.at[k], other)

    def reduce_away(k):
        arrived(p.at[k, 1], swap_sem.at[k])
        away[k] = reduced(k, 1 - z)
        if k == 1:
            short[0] = away[k].astype(BF16)
        if k < SUB - 1:
            swap_chips(k).start()

    def reduce_keep(k):
        keep[k] = reduced(k, z)

    def late_away(k):
        arrived(late.at[1], swap_sem.at[SUB])
        short[1] = (away[k] + reduced_late(k, 1 - z)).astype(BF16)
        swap_chips(k).start()

    def late_keep(k):
        keep[k] = keep[k] + reduced_late(k, z)
        result(k).start()

    def finish(k):
        there = short_far if k else far
        arrived(there, chip_sem.at[k])
        keep[k] = keep[k] + there[...].astype(F32)
        result(k).start()

    def result(k):
        return pltpu.make_async_copy(keep.at[k], out.at[k], out_sem)

    load()

    barrier = pltpu.get_barrier_semaphore()
    for device in (right, left, across, twin, other):
        pl.semaphore_signal(barrier, inc=1, device_id=device, device_id_type=MESH)
    pl.semaphore_wait(barrier, 5)

    start(*raw(0, 0))
    start(to_other(0), to_other(1), to_other(2), to_twin())
    pack(0)
    start(*raw(0, 1))
    start(*raw(1, 0))
    pack(1)
    start(*raw(1, 1))
    arrived(near, load_sem.at[SUB])
    add_to_partial(0, 0)
    add_to_partial(0, 1)
    pack(2)
    send_diagonals()
    add_to_partial(1, 0)
    add_to_partial(1, 1)
    merge(0, 0)
    merge(0, 1)
    start(*gather_rest(0))
    start(*raw(2, 0), *raw(2, 1))
    merge(1, 0)
    merge(1, 1)
    start(*gather_rest(1))
    start_relay(0, 0)
    start_relay(0, 1)
    pass_modes(0)
    merge_diagonals()
    add_to_partial(2, 0)
    add_to_partial(2, 1)
    pass_modes(1)
    start_relay(1, 0)
    start_relay(1, 1)
    arrived(vo, load_sem.at[SUB + 1])
    arrived(vt.at[:, 0], modes_sem.at[SUB])
    project_all(0)
    merge(2, 0)
    merge(2, 1)
    start(*gather_rest(2))
    reduce_away(0)
    reduce_keep(0)
    pass_modes(2)
    project_all(1)
    start_relay(2, 0)
    start_relay(2, 1)
    reduce_away(1)
    reduce_keep(1)
    project_mine(2)
    project_sides(2)
    finish(0)
    reduce_away(2)
    project_far(2)
    reduce_keep(2)
    late_away(2)
    late_keep(2)
    finish(1)

    for i, ref in enumerate((m, vz, diag.at[pl.ds(0, 3)], m)):
        arrived(ref, sent.at[i])

    @pl.when(core == 0)
    def _():
        arrived(vz, sent.at[4])

    arrived(vz, sent.at[5])
    arrived(inbox.at[0, pl.ds(0, 5)], sent.at[6])
    arrived(keep, out_sem)
    arrived(out_far, chip_sem.at[SUB - 1])


def shards(schur, modes, counts):
    dma = pltpu.SemaphoreType.DMA
    reduced, far = pl.pallas_call(
        kernel,
        out_shape=(jax.ShapeDtypeStruct((SUB, Q, N), F32), jax.ShapeDtypeStruct((Q, N), BF16)),
        in_specs=[ANY, ANY],
        out_specs=(ANY, ANY),
        scratch_shapes=[
            pltpu.VMEM((SUB, N, N), BF16),
            pltpu.VMEM((SUB, N, N), BF16),
            pltpu.VMEM((SUB, N, N), BF16),
            pltpu.VMEM((SUB, 2, Q, N), BF16),
            pltpu.VMEM((SUB, 6, Q, N), BF16),
            pltpu.VMEM((SUB, 2, Q, N), BF16),
            pltpu.VMEM((SUB, 2, N, N), BF16),
            pltpu.VMEM((RING, 16, Q), BF16),
            pltpu.VMEM((16, Q), F32),
            pltpu.VMEM((8, N), F32),
            pltpu.VMEM((SUB, N, N), BF16),
            pltpu.VMEM((SUB, 2, N, N), BF16),
            pltpu.VMEM((SUB, N, N), BF16),
            pltpu.VMEM((SUB, 2, N, N), BF16),
            pltpu.VMEM((2, Q, N), BF16),
            pltpu.VMEM((SUB, Q, N), F32),
            pltpu.VMEM((SUB, Q, N), F32),
            pltpu.VMEM((Q, N), F32),
            pltpu.VMEM((2, Q, N), BF16),
            pltpu.VMEM((Q, N), BF16),
            dma((SUB + 2,)),
            dma((7,)),
            dma((SUB, 4)),
            dma,
            dma((SUB, 4)),
            dma((2 * SUB + 1,)),
            dma((SUB + 1,)),
            dma((SUB,)),
            dma,
        ],
        compiler_params=pltpu.CompilerParams(
            collective_id=0, has_side_effects=True, vmem_limit_bytes=52 << 20
        ),
        cost_estimate=pl.CostEstimate(flops=5 * SUB * 2 * N**3, bytes_accessed=8 << 20, transcendentals=0),
        name="merge_and_project",
    )(schur, modes)
    reduced += jnp.pad(far.astype(F32)[None], ((SUB - 1, 0), (0, 0), (0, 0)))
    row = lax.axis_index("blk") * Q + lax.broadcasted_iota(jnp.int32, reduced.shape, 1)
    column = lax.broadcasted_iota(jnp.int32, reduced.shape, 2)
    kept = counts[0][:, None, None]
    return jnp.where((row < kept) & (column < kept), reduced, 0.0)[None]


def solution(mesh):
    placed = (P("leaf", None, "blk", None), P("leaf", None, "blk", None), P("leaf", None))
    return jax.shard_map(
        shards, mesh=mesh, in_specs=placed, out_specs=P("leaf", None, "blk", None), check_vma=False
    )
```

```python
import jax
import jax.numpy as jnp
from jax import lax
from jax.experimental import pallas as pl
from jax.experimental.pallas import tpu as pltpu
from jax.sharding import PartitionSpec as P

MESH = pl.DeviceIdType.MESH
ANY = pl.BlockSpec(memory_space=pl.ANY)
F32 = jnp.float32
BF16 = jnp.bfloat16

SUB = 3
N = 512
Q = 128
RING = 4


def dot(a, b):
    return jnp.dot(a, b, preferred_element_type=F32)


def dot_rows(a, b):
    return lax.dot_general(a, b, (((0,), (0,)), ((), ())), preferred_element_type=F32)


def kernel(
    schur, modes, out, out_far,
    db, ob, qp, near, inbox, part, m, diag, dg, halves, vo, vt, vz, p, late, keep, away, far, away_last,
    load_sem, sent, raw_sem, diag_sem, all_sem, modes_sem, swap_sem, chip_sem, out_sem,
):
    leaf = lax.axis_index("leaf")
    blk = lax.axis_index("blk")
    x = lax.rem(leaf, RING)
    base = leaf - x
    z, core = blk // 2, lax.rem(blk, 2)
    x1, x2, x3 = (lax.rem(x + i, RING) for i in (1, 2, 3))
    right, across, left = ((base + i, blk) for i in (x1, x2, x3))
    twin = (leaf, z * 2 + 1 - core)
    other = (leaf, (1 - z) * 2 + core)

    def columns(i):
        return pl.ds(pl.multiple_of(lax.rem(blk + i, 4) * N, N), N)

    def quarter(d):
        return pl.ds(pl.multiple_of(d * Q, Q), Q)

    def remote(src, dst, send, recv, to):
        return pltpu.make_async_remote_copy(
            src_ref=src, dst_ref=dst, send_sem=send, recv_sem=recv, device_id=to, device_id_type=MESH
        )

    def arrived(ref, sem):
        pltpu.make_async_copy(ref, ref, sem).wait()

    def start(*copies):
        for c in copies:
            c.start()

    def load():
        for k in range(SUB):
            for i, dst in ((0, db), (2, ob)):
                pltpu.make_async_copy(schur.at[0, k, :, columns(i)], dst.at[k], load_sem.at[k]).start()
        for i, d in enumerate((x, x1)):
            pltpu.make_async_copy(schur.at[0, :, quarter(d), columns(1)], near.at[:, i], load_sem.at[SUB]).start()
        pltpu.make_async_copy(modes.at[0], vo, load_sem.at[SUB + 1]).start()

    def raw(k, t):
        def send(i, d, sem, to):
            src = qp.at[k, quarter(d)] if t else schur.at[0, k, quarter(d), columns(1)]
            return remote(src, inbox.at[k, i], sent.at[0], raw_sem.at[k, sem], to)

        if t:
            return send(3, x2, 2, left), send(4, x1, 3, right)
        return send(0, x2, 0, right), send(1, x3, 1, left)

    def partial(k, t):
        dst = inbox.at[k, 5 if t else 2]
        return remote(part.at[k, t], dst, sent.at[1], raw_sem.at[k, 3 if t else 1], left if t else right)

    def places(blocks):
        row = jnp.concatenate([lax.broadcasted_iota(jnp.int32, (Q, N), 0) + d * Q for d in blocks], axis=0)
        return row, lax.broadcasted_iota(jnp.int32, row.shape, 1)

    def pack(k):
        arrived(p.at[k], load_sem.at[k])
        row, column = places(range(4))
        qp[k] = jnp.where(column > row, db[k], ob[k])

    def send_diagonals():
        row = lax.broadcasted_iota(jnp.int32, (Q, Q), 0)
        column = lax.broadcasted_iota(jnp.int32, (Q, Q), 1)
        for k in range(SUB):
            for r in range(4):
                own = db[k, r * Q : (r + 1) * Q, r * Q : (r + 1) * Q].astype(F32)
                dg[4 * k + r : 4 * k + r + 1, :] = jnp.sum(jnp.where(row == column, own, 0.0), axis=0, keepdims=True)
        diag[x] = dg[...].astype(BF16)
        start(*diagonals())

    def diagonals():
        return [remote(diag.at[x], diag.at[x], sent.at[2], diag_sem, to) for to in (right, left, across)]

    def merge_diagonals():
        arrived(diag.at[pl.ds(0, 3)], diag_sem)
        t = [diag[i].astype(F32) for i in range(RING)]
        dg[...] = ((t[0] + t[1]) + (t[2] + t[3])).astype(BF16).astype(F32) * 0.5
        for k in range(SUB):
            for r in range(4):
                halves[k : k + 1, r * Q : (r + 1) * Q] = dg[4 * k + r : 4 * k + r + 1, :]

    def add_to_partial(k, t):
        arrived(inbox.at[k, 3 * t], raw_sem.at[k, 2 * t])
        own = qp[k, quarter(x3), :] if t else near[k, 1]
        part[k, t] = (inbox[k, 3 * t].astype(F32) + own.astype(F32)).astype(BF16)
        partial(k, t).start()

    def merge(k, t):
        two = pl.ds(3 * t + 1, 2)
        arrived(inbox.at[k, two], raw_sem.at[k, 2 * t + 1])
        own = qp[k, quarter(x), :] if t else near[k, 0]
        total = inbox[k, 3 * t + 2].astype(F32) + inbox[k, 3 * t + 1].astype(F32) + own.astype(F32)
        m[k, t, quarter(x), :] = total.astype(BF16)
        gather(k, t, t, t).start()

    def gather(k, t, side, sem):
        ref = m.at[k, t, quarter(x)]
        return remote(ref, ref, sent.at[0], all_sem.at[k, sem], left if side else right)

    def gather_rest(k):
        return gather(k, 1, 0, 2), gather(k, 0, 1, 2)

    def start_relay(k, t):
        ref = m.at[k, t, quarter(x1 if t else x3)]
        arrived(ref, all_sem.at[k, t])
        remote(ref, ref, sent.at[1], all_sem.at[k, 3], left if t else right).start()

    def gathered_near(k):
        arrived(inbox.at[k, pl.ds(0, 2)], all_sem.at[k, 2])

    def gathered_far(k):
        arrived(inbox.at[k, pl.ds(0, 2)], all_sem.at[k, 3])

    def to_other(k):
        return remote(modes.at[0, k], vz.at[k], sent.at[3], modes_sem.at[k], other)

    def to_twin():
        return remote(modes.at[0], vt.at[:, 0], sent.at[3], modes_sem.at[SUB], twin)

    def pass_modes(k):
        arrived(vz.at[k], modes_sem.at[k])

        @pl.when(core == 0)
        def _():
            remote(vz.at[k], vt.at[k, 1], sent.at[4], modes_sem.at[SUB + 1 + k], twin).start()

    def modes_here(k):
        @pl.when(core == 1)
        def _():
            arrived(vt.at[k, 1], modes_sem.at[SUB + 1 + k])

    def upper(k, blocks, both):
        row, column = places(blocks)
        zero = jnp.zeros_like(both)
        half = jnp.broadcast_to(halves[k : k + 1, :], both.shape).astype(BF16)
        own = jnp.where(column > row, both, jnp.where(column == row, half, zero))
        opposite = jnp.where(column < row, both, jnp.where(column == row, both * 0.5, zero))
        return own, opposite

    def project(k, blocks, following, both):
        own, opposite = upper(k, blocks, both)
        return (dot(following, vt[k, core]) + dot(own, vo[k]) + dot(opposite, vz[k])).astype(BF16)

    def project_blocks(k, *blocks):
        following, both = (jnp.concatenate([m[k, t, quarter(d), :] for d in blocks], axis=0) for t in range(2))
        return project(k, blocks, following, both)

    def swap(k):
        return remote(p.at[k, 0], p.at[k, 1], sent.at[5], swap_sem.at[k], twin)

    def swap_block(k, d):
        return remote(p.at[k, 0, quarter(d)], p.at[k, 1, quarter(d)], sent.at[5], swap_sem.at[k], twin)

    def swap_late():
        return remote(late.at[0], late.at[1], sent.at[5], swap_sem.at[SUB], twin)

    def project_all(k):
        gathered_near(k)
        gathered_far(k)
        modes_here(k)
        p[k, 0] = project(k, range(4), m[k, 0], m[k, 1])
        swap(k).start()

    def project_mine(k):
        modes_here(k)
        p[k, 0, quarter(x), :] = project_blocks(k, x)
        swap_block(k, x).start()
        for i in range(2):
            p[k, i, quarter(x2), :] = jnp.zeros((Q, N), BF16)

    def project_sides(k):
        gathered_near(k)
        sides = project_blocks(k, x1, x3)
        p[k, 0, quarter(x1), :] = sides[:Q]
        p[k, 0, quarter(x3), :] = sides[Q:]
        start(swap_block(k, x1), swap_block(k, x3))

    def project_far(k):
        gathered_far(k)
        late[0] = project_blocks(k, x2)
        swap_late().start()

    def slab(i):
        return pl.ds(pl.multiple_of((2 * i + core) * Q, Q), Q)

    def reduced(k, i):
        total = dot_rows(vo[k, :, slab(i)], p[k, 0]) + dot_rows(p[k, 0, :, slab(i)], vo[k])
        return total + dot_rows(vt[k, 0, :, slab(i)], p[k, 1]) + dot_rows(p[k, 1, :, slab(i)], vt[k, 0])

    def reduced_late(k, i):
        total = dot_rows(vo[k, quarter(x2), slab(i)], late[0]) + dot_rows(late[0, :, slab(i)], vo[k, quarter(x2), :])
        total += dot_rows(vt[k, 0, quarter(x2), slab(i)], late[1])
        return total + dot_rows(late[1, :, slab(i)], vt[k, 0, quarter(x2), :])

    def swap_chips(k):
        src, dst = (away_last, out_far) if k == SUB - 1 else (away.at[k], far.at[k])
        return remote(src, dst, sent.at[6], chip_sem.at[k], other)

    def reduce_away(k):
        arrived(inbox.at[0, pl.ds(0, 3)] if k == SUB - 1 else p.at[k, 1], swap_sem.at[k])
        away[k] = reduced(k, 1 - z)
        if k < SUB - 1:
            swap_chips(k).start()

    def reduce_keep(k):
        keep[k] = reduced(k, z)

    def late_away(k):
        arrived(late.at[1], swap_sem.at[SUB])
        away_last[...] = (away[k] + reduced_late(k, 1 - z)).astype(BF16)
        swap_chips(k).start()

    def late_keep(k):
        keep[k] = keep[k] + reduced_late(k, z)
        result(k).start()

    def finish(k):
        arrived(far.at[k], chip_sem.at[k])
        keep[k] = keep[k] + far[k]
        result(k).start()

    def result(k):
        return pltpu.make_async_copy(keep.at[k], out.at[k], out_sem)

    load()

    barrier = pltpu.get_barrier_semaphore()
    for device in (right, left, across, twin, other):
        pl.semaphore_signal(barrier, inc=1, device_id=device, device_id_type=MESH)
    pl.semaphore_wait(barrier, 5)

    start(*raw(0, 0))
    start(to_other(0), to_other(1), to_other(2), to_twin())
    pack(0)
    start(*raw(0, 1))
    start(*raw(1, 0))
    pack(1)
    start(*raw(1, 1))
    arrived(near, load_sem.at[SUB])
    add_to_partial(0, 0)
    add_to_partial(0, 1)
    pack(2)
    send_diagonals()
    add_to_partial(1, 0)
    add_to_partial(1, 1)
    merge(0, 0)
    merge(0, 1)
    start(*gather_rest(0))
    start(*raw(2, 0), *raw(2, 1))
    merge(1, 0)
    merge(1, 1)
    start(*gather_rest(1))
    start_relay(0, 0)
    start_relay(0, 1)
    pass_modes(0)
    merge_diagonals()
    add_to_partial(2, 0)
    add_to_partial(2, 1)
    pass_modes(1)
    start_relay(1, 0)
    start_relay(1, 1)
    arrived(vo, load_sem.at[SUB + 1])
    arrived(vt.at[:, 0], modes_sem.at[SUB])
    project_all(0)
    merge(2, 0)
    merge(2, 1)
    start(*gather_rest(2))
    reduce_away(0)
    reduce_keep(0)
    pass_modes(2)
    project_all(1)
    start_relay(2, 0)
    start_relay(2, 1)
    reduce_away(1)
    reduce_keep(1)
    project_mine(2)
    project_sides(2)
    finish(0)
    reduce_away(2)
    project_far(2)
    reduce_keep(2)
    late_away(2)
    late_keep(2)
    finish(1)

    for i, ref in enumerate((m, vz, diag.at[pl.ds(0, 3)], m)):
        arrived(ref, sent.at[i])

    @pl.when(core == 0)
    def _():
        arrived(vz, sent.at[4])

    arrived(vz, sent.at[5])
    arrived(inbox.at[0, pl.ds(0, 5)], sent.at[6])
    arrived(keep, out_sem)
    arrived(out_far, chip_sem.at[SUB - 1])


def shards(schur, modes, counts):
    dma = pltpu.SemaphoreType.DMA
    reduced, far = pl.pallas_call(
        kernel,
        out_shape=(jax.ShapeDtypeStruct((SUB, Q, N), F32), jax.ShapeDtypeStruct((Q, N), BF16)),
        in_specs=[ANY, ANY],
        out_specs=(ANY, ANY),
        scratch_shapes=[
            pltpu.VMEM((SUB, N, N), BF16),
            pltpu.VMEM((SUB, N, N), BF16),
            pltpu.VMEM((SUB, N, N), BF16),
            pltpu.VMEM((SUB, 2, Q, N), BF16),
            pltpu.VMEM((SUB, 6, Q, N), BF16),
            pltpu.VMEM((SUB, 2, Q, N), BF16),
            pltpu.VMEM((SUB, 2, N, N), BF16),
            pltpu.VMEM((RING, 16, Q), BF16),
            pltpu.VMEM((16, Q), F32),
            pltpu.VMEM((8, N), F32),
            pltpu.VMEM((SUB, N, N), BF16),
            pltpu.VMEM((SUB, 2, N, N), BF16),
            pltpu.VMEM((SUB, N, N), BF16),
            pltpu.VMEM((SUB, 2, N, N), BF16),
            pltpu.VMEM((2, Q, N), BF16),
            pltpu.VMEM((SUB, Q, N), F32),
            pltpu.VMEM((SUB, Q, N), F32),
            pltpu.VMEM((SUB - 1, Q, N), F32),
            pltpu.VMEM((Q, N), BF16),
            dma((SUB + 2,)),
            dma((7,)),
            dma((SUB, 4)),
            dma,
            dma((SUB, 4)),
            dma((2 * SUB + 1,)),
            dma((SUB + 1,)),
            dma((SUB,)),
            dma,
        ],
        compiler_params=pltpu.CompilerParams(
            collective_id=0, has_side_effects=True, vmem_limit_bytes=52 << 20
        ),
        cost_estimate=pl.CostEstimate(flops=5 * SUB * 2 * N**3, bytes_accessed=8 << 20, transcendentals=0),
        name="merge_and_project",
    )(schur, modes)
    reduced += jnp.pad(far.astype(F32)[None], ((SUB - 1, 0), (0, 0), (0, 0)))
    row = lax.axis_index("blk") * Q + lax.broadcasted_iota(jnp.int32, reduced.shape, 1)
    column = lax.broadcasted_iota(jnp.int32, reduced.shape, 2)
    kept = counts[0][:, None, None]
    return jnp.where((row < kept) & (column < kept), reduced, 0.0)[None]


def solution(mesh):
    placed = (P("leaf", None, "blk", None), P("leaf", None, "blk", None), P("leaf", None))
    return jax.shard_map(
        shards, mesh=mesh, in_specs=placed, out_specs=P("leaf", None, "blk", None), check_vma=False
    )
```

```python
import jax
import jax.numpy as jnp
from jax import lax
from jax.experimental import pallas as pl
from jax.experimental.pallas import tpu as pltpu
from jax.sharding import PartitionSpec as P

MESH = pl.DeviceIdType.MESH
ANY = pl.BlockSpec(memory_space=pl.ANY)
F32 = jnp.float32
BF16 = jnp.bfloat16

SUB = 3
N = 512
Q = 128
RING = 4


def dot(a, b):
    return jnp.dot(a, b, preferred_element_type=F32)


def dot_rows(a, b):
    return lax.dot_general(a, b, (((0,), (0,)), ((), ())), preferred_element_type=F32)


def kernel(
    schur, modes, out, out_far,
    db, ob, qp, near, inbox, part, m, diag, dg, halves, vo, vt, vz, p, late, keep, away, far, away_last,
    load_sem, sent, raw_sem, diag_sem, all_sem, modes_sem, swap_sem, chip_sem, out_sem,
):
    leaf = lax.axis_index("leaf")
    blk = lax.axis_index("blk")
    x = lax.rem(leaf, RING)
    base = leaf - x
    z, core = blk // 2, lax.rem(blk, 2)
    x1, x2, x3 = (lax.rem(x + i, RING) for i in (1, 2, 3))
    right, across, left = ((base + i, blk) for i in (x1, x2, x3))
    twin = (leaf, z * 2 + 1 - core)
    other = (leaf, (1 - z) * 2 + core)

    def columns(i):
        return pl.ds(pl.multiple_of(lax.rem(blk + i, 4) * N, N), N)

    def quarter(d):
        return pl.ds(pl.multiple_of(d * Q, Q), Q)

    def remote(src, dst, send, recv, to):
        return pltpu.make_async_remote_copy(
            src_ref=src, dst_ref=dst, send_sem=send, recv_sem=recv, device_id=to, device_id_type=MESH
        )

    def arrived(ref, sem):
        pltpu.make_async_copy(ref, ref, sem).wait()

    def start(*copies):
        for c in copies:
            c.start()

    def load():
        for k in range(SUB):
            for i, dst in ((0, db), (2, ob)):
                pltpu.make_async_copy(schur.at[0, k, :, columns(i)], dst.at[k], load_sem.at[k]).start()
        for i, d in enumerate((x, x1)):
            pltpu.make_async_copy(schur.at[0, :, quarter(d), columns(1)], near.at[:, i], load_sem.at[SUB]).start()
        pltpu.make_async_copy(modes.at[0], vo, load_sem.at[SUB + 1]).start()

    def raw(k, t):
        def send(i, d, sem, to):
            src = qp.at[k, quarter(d)] if t else schur.at[0, k, quarter(d), columns(1)]
            return remote(src, inbox.at[k, i], sent.at[0], raw_sem.at[k, sem], to)

        if t:
            return send(3, x2, 2, left), send(4, x1, 3, right)
        return send(0, x2, 0, right), send(1, x3, 1, left)

    def partial(k, t):
        dst = inbox.at[k, 5 if t else 2]
        return remote(part.at[k, t], dst, sent.at[1], raw_sem.at[k, 3 if t else 1], left if t else right)

    def places(blocks):
        row = jnp.concatenate([lax.broadcasted_iota(jnp.int32, (Q, N), 0) + d * Q for d in blocks], axis=0)
        return row, lax.broadcasted_iota(jnp.int32, row.shape, 1)

    def pack(k):
        arrived(p.at[k], load_sem.at[k])
        row, column = places(range(4))
        qp[k] = jnp.where(column > row, db[k], ob[k])

    def send_diagonals():
        row = lax.broadcasted_iota(jnp.int32, (Q, Q), 0)
        column = lax.broadcasted_iota(jnp.int32, (Q, Q), 1)
        for k in range(SUB):
            for r in range(4):
                own = db[k, r * Q : (r + 1) * Q, r * Q : (r + 1) * Q].astype(F32)
                dg[4 * k + r : 4 * k + r + 1, :] = jnp.sum(jnp.where(row == column, own, 0.0), axis=0, keepdims=True)
        diag[x] = dg[...].astype(BF16)
        start(*diagonals())

    def diagonals():
        return [remote(diag.at[x], diag.at[x], sent.at[2], diag_sem, to) for to in (right, left, across)]

    def merge_diagonals():
        arrived(diag.at[pl.ds(0, 3)], diag_sem)
        t = [diag[i].astype(F32) for i in range(RING)]
        dg[...] = ((t[0] + t[1]) + (t[2] + t[3])).astype(BF16).astype(F32) * 0.5
        for k in range(SUB):
            for r in range(4):
                halves[k : k + 1, r * Q : (r + 1) * Q] = dg[4 * k + r : 4 * k + r + 1, :]

    def add_to_partial(k, t):
        arrived(inbox.at[k, 3 * t], raw_sem.at[k, 2 * t])
        own = qp[k, quarter(x3), :] if t else near[k, 1]
        part[k, t] = (inbox[k, 3 * t].astype(F32) + own.astype(F32)).astype(BF16)
        partial(k, t).start()

    def merge(k, t):
        two = pl.ds(3 * t + 1, 2)
        arrived(inbox.at[k, two], raw_sem.at[k, 2 * t + 1])
        own = qp[k, quarter(x), :] if t else near[k, 0]
        total = inbox[k, 3 * t + 2].astype(F32) + inbox[k, 3 * t + 1].astype(F32) + own.astype(F32)
        m[k, t, quarter(x), :] = total.astype(BF16)
        gather(k, t, t, t).start()

    def gather(k, t, side, sem):
        ref = m.at[k, t, quarter(x)]
        return remote(ref, ref, sent.at[0], all_sem.at[k, sem], left if side else right)

    def gather_rest(k):
        return gather(k, 1, 0, 2), gather(k, 0, 1, 2)

    def start_relay(k, t):
        ref = m.at[k, t, quarter(x1 if t else x3)]
        arrived(ref, all_sem.at[k, t])
        remote(ref, ref, sent.at[1], all_sem.at[k, 3], left if t else right).start()

    def gathered_near(k):
        arrived(inbox.at[k, pl.ds(0, 2)], all_sem.at[k, 2])

    def gathered_far(k):
        arrived(inbox.at[k, pl.ds(0, 2)], all_sem.at[k, 3])

    def to_other(k):
        return remote(modes.at[0, k], vz.at[k], sent.at[3], modes_sem.at[k], other)

    def to_twin():
        return remote(modes.at[0], vt.at[:, 0], sent.at[3], modes_sem.at[SUB], twin)

    def pass_modes(k):
        arrived(vz.at[k], modes_sem.at[k])

        @pl.when(core == 0)
        def _():
            remote(vz.at[k], vt.at[k, 1], sent.at[4], modes_sem.at[SUB + 1 + k], twin).start()

    def modes_here(k):
        @pl.when(core == 1)
        def _():
            arrived(vt.at[k, 1], modes_sem.at[SUB + 1 + k])

    def upper(k, blocks, both):
        row, column = places(blocks)
        zero = jnp.zeros_like(both)
        half = jnp.broadcast_to(halves[k : k + 1, :], both.shape).astype(BF16)
        own = jnp.where(column > row, both, jnp.where(column == row, half, zero))
        opposite = jnp.where(column < row, both, jnp.where(column == row, both * 0.5, zero))
        return own, opposite

    def project(k, blocks, following, both):
        own, opposite = upper(k, blocks, both)
        return (dot(following, vt[k, core]) + dot(own, vo[k]) + dot(opposite, vz[k])).astype(BF16)

    def project_blocks(k, *blocks):
        following, both = (jnp.concatenate([m[k, t, quarter(d), :] for d in blocks], axis=0) for t in range(2))
        return project(k, blocks, following, both)

    def swap(k):
        return remote(p.at[k, 0], p.at[k, 1], sent.at[5], swap_sem.at[k], twin)

    def swap_block(k, d):
        return remote(p.at[k, 0, quarter(d)], p.at[k, 1, quarter(d)], sent.at[5], swap_sem.at[k], twin)

    def swap_late():
        return remote(late.at[0], late.at[1], sent.at[5], swap_sem.at[SUB], twin)

    def project_all(k):
        gathered_near(k)
        gathered_far(k)
        modes_here(k)
        p[k, 0] = project(k, range(4), m[k, 0], m[k, 1])
        swap(k).start()

    def project_mine(k):
        modes_here(k)
        p[k, 0, quarter(x), :] = project_blocks(k, x)
        swap_block(k, x).start()
        for i in range(2):
            p[k, i, quarter(x2), :] = jnp.zeros((Q, N), BF16)

    def project_sides(k):
        gathered_near(k)
        sides = project_blocks(k, x1, x3)
        p[k, 0, quarter(x1), :] = sides[:Q]
        p[k, 0, quarter(x3), :] = sides[Q:]
        start(swap_block(k, x1), swap_block(k, x3))

    def project_far(k):
        gathered_far(k)
        late[0] = project_blocks(k, x2)
        swap_late().start()

    def slab(i):
        return pl.ds(pl.multiple_of((2 * i + core) * Q, Q), Q)

    def reduced(k, i):
        total = dot_rows(vo[k, :, slab(i)], p[k, 0]) + dot_rows(p[k, 0, :, slab(i)], vo[k])
        return total + dot_rows(vt[k, 0, :, slab(i)], p[k, 1]) + dot_rows(p[k, 1, :, slab(i)], vt[k, 0])

    def reduced_late(k, i):
        own, there = vo[k, quarter(x2), :], vt[k, 0, quarter(x2), :]
        mine = (vo[k, quarter(x2), slab(i)], late[0, :, slab(i)])
        theirs = (vt[k, 0, quarter(x2), slab(i)], late[1, :, slab(i)])
        rows = jnp.concatenate([*mine, *theirs], axis=0)
        return dot_rows(rows, jnp.concatenate([late[0], own, late[1], there], axis=0))

    def swap_chips(k):
        src, dst = (away_last, out_far) if k == SUB - 1 else (away.at[k], far.at[k])
        return remote(src, dst, sent.at[6], chip_sem.at[k], other)

    def reduce_away(k):
        arrived(inbox.at[0, pl.ds(0, 3)] if k == SUB - 1 else p.at[k, 1], swap_sem.at[k])
        away[k] = reduced(k, 1 - z)
        if k < SUB - 1:
            swap_chips(k).start()

    def reduce_keep(k):
        keep[k] = reduced(k, z)

    def late_away(k):
        arrived(late.at[1], swap_sem.at[SUB])
        away_last[...] = (away[k] + reduced_late(k, 1 - z)).astype(BF16)
        swap_chips(k).start()

    def late_keep(k):
        keep[k] = keep[k] + reduced_late(k, z)
        result(k).start()

    def finish(k):
        arrived(far.at[k], chip_sem.at[k])
        keep[k] = keep[k] + far[k]
        result(k).start()

    def result(k):
        return pltpu.make_async_copy(keep.at[k], out.at[k], out_sem)

    load()

    barrier = pltpu.get_barrier_semaphore()
    for device in (right, left, across, twin, other):
        pl.semaphore_signal(barrier, inc=1, device_id=device, device_id_type=MESH)
    pl.semaphore_wait(barrier, 5)

    start(*raw(0, 0))
    start(to_other(0), to_other(1), to_other(2), to_twin())
    pack(0)
    start(*raw(0, 1))
    start(*raw(1, 0))
    pack(1)
    start(*raw(1, 1))
    arrived(near, load_sem.at[SUB])
    add_to_partial(0, 0)
    add_to_partial(0, 1)
    pack(2)
    send_diagonals()
    add_to_partial(1, 0)
    add_to_partial(1, 1)
    merge(0, 0)
    merge(0, 1)
    start(*gather_rest(0))
    start(*raw(2, 0), *raw(2, 1))
    merge(1, 0)
    merge(1, 1)
    start(*gather_rest(1))
    start_relay(0, 0)
    start_relay(0, 1)
    pass_modes(0)
    merge_diagonals()
    add_to_partial(2, 0)
    add_to_partial(2, 1)
    pass_modes(1)
    start_relay(1, 0)
    start_relay(1, 1)
    arrived(vo, load_sem.at[SUB + 1])
    arrived(vt.at[:, 0], modes_sem.at[SUB])
    project_all(0)
    merge(2, 0)
    merge(2, 1)
    start(*gather_rest(2))
    reduce_away(0)
    reduce_keep(0)
    pass_modes(2)
    project_all(1)
    start_relay(2, 0)
    start_relay(2, 1)
    reduce_away(1)
    reduce_keep(1)
    project_mine(2)
    project_sides(2)
    finish(0)
    reduce_away(2)
    project_far(2)
    reduce_keep(2)
    late_away(2)
    late_keep(2)
    finish(1)

    for i, ref in enumerate((m, vz, diag.at[pl.ds(0, 3)], m)):
        arrived(ref, sent.at[i])

    @pl.when(core == 0)
    def _():
        arrived(vz, sent.at[4])

    arrived(vz, sent.at[5])
    arrived(inbox.at[0, pl.ds(0, 5)], sent.at[6])
    arrived(keep, out_sem)
    arrived(out_far, chip_sem.at[SUB - 1])


def shards(schur, modes, counts):
    dma = pltpu.SemaphoreType.DMA
    reduced, far = pl.pallas_call(
        kernel,
        out_shape=(jax.ShapeDtypeStruct((SUB, Q, N), F32), jax.ShapeDtypeStruct((Q, N), BF16)),
        in_specs=[ANY, ANY],
        out_specs=(ANY, ANY),
        scratch_shapes=[
            pltpu.VMEM((SUB, N, N), BF16),
            pltpu.VMEM((SUB, N, N), BF16),
            pltpu.VMEM((SUB, N, N), BF16),
            pltpu.VMEM((SUB, 2, Q, N), BF16),
            pltpu.VMEM((SUB, 6, Q, N), BF16),
            pltpu.VMEM((SUB, 2, Q, N), BF16),
            pltpu.VMEM((SUB, 2, N, N), BF16),
            pltpu.VMEM((RING, 16, Q), BF16),
            pltpu.VMEM((16, Q), F32),
            pltpu.VMEM((8, N), F32),
            pltpu.VMEM((SUB, N, N), BF16),
            pltpu.VMEM((SUB, 2, N, N), BF16),
            pltpu.VMEM((SUB, N, N), BF16),
            pltpu.VMEM((SUB, 2, N, N), BF16),
            pltpu.VMEM((2, Q, N), BF16),
            pltpu.VMEM((SUB, Q, N), F32),
            pltpu.VMEM((SUB, Q, N), F32),
            pltpu.VMEM((SUB - 1, Q, N), F32),
            pltpu.VMEM((Q, N), BF16),
            dma((SUB + 2,)),
            dma((7,)),
            dma((SUB, 4)),
            dma,
            dma((SUB, 4)),
            dma((2 * SUB + 1,)),
            dma((SUB + 1,)),
            dma((SUB,)),
            dma,
        ],
        compiler_params=pltpu.CompilerParams(
            collective_id=0, has_side_effects=True, vmem_limit_bytes=52 << 20
        ),
        cost_estimate=pl.CostEstimate(flops=5 * SUB * 2 * N**3, bytes_accessed=8 << 20, transcendentals=0),
        name="merge_and_project",
    )(schur, modes)
    reduced += jnp.pad(far.astype(F32)[None], ((SUB - 1, 0), (0, 0), (0, 0)))
    row = lax.axis_index("blk") * Q + lax.broadcasted_iota(jnp.int32, reduced.shape, 1)
    column = lax.broadcasted_iota(jnp.int32, reduced.shape, 2)
    kept = counts[0][:, None, None]
    return jnp.where((row < kept) & (column < kept), reduced, 0.0)[None]


def solution(mesh):
    placed = (P("leaf", None, "blk", None), P("leaf", None, "blk", None), P("leaf", None))
    return jax.shard_map(
        shards, mesh=mesh, in_specs=placed, out_specs=P("leaf", None, "blk", None), check_vma=False
    )
```
